32 devices in a mesh: dp: 8 (over y, x, core), feat: 4 (over z).
Axes of the slice: x: 2, y: 2, z: 4, core: 2. Of those that a mesh axis runs over, the one named last changes fastest.
Arguments:
- features: bfloat16 [2048, 16384], P('dp', 'feat'), may hold values from -6 to 6
- gate: float32 [2048], P('dp'), may hold values from 0.1 to 1
- bias: float32 [16384], P('feat'), may hold values from -3 to 3
- down_weight: bfloat16 [16384, 512], P('feat', 'dp'), may hold values from -0.046875 to 0.046875
- up_weight: bfloat16 [512, 16384], P('dp', 'feat'), may hold values from -0.25 to 0.25
- cotangent: bfloat16 [2048, 16384], P(('dp', 'feat')), may hold values from -0.75 to 0.75
Outputs:
- cross_out: bfloat16 [2048, 16384], P(('dp', 'feat'))
- grad_up: float32 [512, 16384], P('dp', 'feat')
- grad_down: float32 [16384, 512], P('feat', 'dp')
- grad_bias: float32 [16384], P('feat')
- grad_in: bfloat16 [2048, 16384], P('dp', 'feat')
The draws below stay inside these ranges and needn't reach their ends.
All inputs are finite; a program needn't handle non-finite values.
Results may differ from the reference program's by a relative error of at most 0.0049.
Values may be sent and summed in bfloat16 or wider, within the bound.
A program may use at most 128 MiB of HBM per device.

```python
import math
import jax
import jax.numpy as jnp
from jax import lax

D = 16384
RANK = 512
ROWS = 256
SAMPLES = 2048
N_DP = 8


def level_of(rng, dims, split, least, top_value):
    level, own = 1.0, jax.random.fold_in(rng, 6)
    for axis_at, parts in split:
        steps = jnp.exp(jax.random.uniform(jax.random.fold_in(own, axis_at), (parts,), jnp.float32, least / len(split), top_value / len(split)))
        level = level * jnp.repeat(steps, dims[axis_at] // parts).reshape([-1 if axis == axis_at else 1 for axis in range(len(dims))])
    return level


def normal_values(stream_key, dims, deviation, limit, pieces=(), dtype=jnp.bfloat16):
    gain = level_of(stream_key, dims, pieces, -0.22, 0.18) if pieces else 1.0
    result = jax.random.normal(stream_key, dims, jnp.float32) * deviation * gain
    return jnp.minimum(jnp.maximum(result, -limit), limit).astype(dtype)


def setup_inputs(seed: int = 0) -> dict:
    streams_of = jax.random.split(jax.random.key(seed), 7)
    features = normal_values(streams_of[0], (SAMPLES, D), 1.0, 6.0, ((0, 8), (1, 4)))
    gate = jnp.clip(jnp.exp(math.log(1.0) - 2.3025851 * jax.random.uniform(streams_of[1], (SAMPLES,), jnp.float32) ** level_of(streams_of[1], (SAMPLES,), ((0, 8),), -0.2, 0.2)), 0.1, 1.0)
    bias = normal_values(streams_of[2], (D,), 0.5, 3.0, ((0, 4),), jnp.float32)
    down_weight = normal_values(streams_of[3], (D, RANK), D ** -0.5, 0.046875, ((0, 4), (1, 8)))
    up_weight = normal_values(streams_of[4], (RANK, D), RANK ** -0.5, 0.25, ((0, 8), (1, 4)))
    cotangent = normal_values(streams_of[5], (SAMPLES, D), 0.125, 0.75, ((0, 32),))
    return {"features": features, "gate": gate, "bias": bias, "down_weight": down_weight, "up_weight": up_weight, "cotangent": cotangent}


def reference(features, gate, bias, down_weight, up_weight, cotangent):
    feat_blocks = features.reshape(N_DP, ROWS, D)
    gate_blocks = gate.reshape(N_DP, ROWS)
    cot_blocks = cotangent.reshape(N_DP, ROWS, D)

    def one_group(carry, block):
        acc_up, acc_down, acc_bias = carry
        xin, gates, cot = block
        h = jnp.dot(xin, down_weight, preferred_element_type=jnp.float32)
        low = h.astype(jnp.bfloat16)
        proj = jnp.dot(low, up_weight, preferred_element_type=jnp.float32)
        scale = gates[:, None] * proj + bias[None, :]
        xf = xin.astype(jnp.float32)
        cross = (xf * (1.0 + scale)).astype(jnp.bfloat16)
        dy = cot.astype(jnp.float32)
        pre_grad = dy * xf
        acc_bias = acc_bias + jnp.sum(pre_grad, axis=0)
        gated_grad = (gates[:, None] * pre_grad).astype(jnp.bfloat16)
        acc_up = acc_up + jnp.dot(low.T, gated_grad, preferred_element_type=jnp.float32)
        rank_grad = jnp.dot(gated_grad, up_weight.T, preferred_element_type=jnp.float32)
        low_grad = rank_grad.astype(jnp.bfloat16)
        acc_down = acc_down + jnp.dot(xin.T, low_grad, preferred_element_type=jnp.float32)
        back = jnp.dot(low_grad, down_weight.T, preferred_element_type=jnp.float32)
        grad_in = (dy * (1.0 + scale) + back).astype(jnp.bfloat16)
        return (acc_up, acc_down, acc_bias), (cross, grad_in)

    start = (jnp.zeros((RANK, D), jnp.float32), jnp.zeros((D, RANK), jnp.float32), jnp.zeros((D,), jnp.float32))
    (grad_up, grad_down, grad_bias), (cross, grad_in) = lax.scan(one_group, start, (feat_blocks, gate_blocks, cot_blocks))
    return cross.reshape(SAMPLES, D), grad_up, grad_down, grad_bias, grad_in.reshape(SAMPLES, D)
```

```python
import functools

import jax
import jax.numpy as jnp
from jax import lax
from jax.experimental import pallas as pl
from jax.experimental.pallas import tpu as pltpu
from jax.sharding import PartitionSpec as P

MESH = pl.DeviceIdType.MESH
F32 = jnp.float32
BF16 = jnp.bfloat16
NT = (((1,), (1,)), ((), ()))
TILE = 512
CHUNKS = 4


def rank_total(partial_value):
    return lax.psum(partial_value, "feat").astype(jnp.bfloat16)


def plain_form(features, gate, bias, down_weight, up_weight, cotangent):
    down_full, up_full = (
        lax.all_gather(down_weight, "dp", axis=1, tiled=True),
        lax.all_gather(up_weight, "dp", axis=0, tiled=True),
    )
    low = rank_total(jnp.dot(features, down_full, preferred_element_type=jnp.float32))
    proj = jnp.dot(low, up_full, preferred_element_type=jnp.float32)
    scale = gate[:, None] * proj + bias[None, :]
    xfloat = features.astype(jnp.float32)
    cross = (xfloat * (1.0 + scale)).astype(jnp.bfloat16)
    cross_out = lax.all_to_all(cross, "feat", split_axis=0, concat_axis=1, tiled=True)
    upstream = lax.all_to_all(cotangent, "feat", split_axis=1, concat_axis=0, tiled=True).astype(
        jnp.float32
    )
    pre_grad = upstream * xfloat
    bias_terms = jnp.sum(pre_grad, axis=0)
    gated_grad = (gate[:, None] * pre_grad).astype(jnp.bfloat16)
    contract_first = (((0,), (0,)), ((), ()))
    rank_grad = lax.dot_general(gated_grad, up_full, NT, preferred_element_type=jnp.float32)
    low_grad = rank_total(rank_grad)
    grad_up = lax.psum_scatter(
        lax.dot_general(low, gated_grad, contract_first, preferred_element_type=jnp.float32),
        "dp",
        scatter_dimension=0,
        tiled=True,
    )
    down_terms = lax.dot_general(
        features, low_grad, contract_first, preferred_element_type=jnp.float32
    )
    grad_down = lax.psum_scatter(down_terms, "dp", scatter_dimension=1, tiled=True)
    grad_bias = lax.psum(bias_terms, "dp")
    back = lax.dot_general(low_grad, down_full, NT, preferred_element_type=jnp.float32)
    grad_in = (upstream * (1.0 + scale) + back).astype(jnp.bfloat16)
    return (cross_out, grad_up, grad_down, grad_bias, grad_in)


def kernel(
    n_dp, n_feat, steps,
    x, cot, down, up, gate, bias,
    cross_out, grad_up, grad_down, grad_bias, grad_in,
    cot_v, d_full, u_full, one_scale, gated, cross,
    acc_up, acc_down, out_up, out_down, in_up, in_down,
    h_part, h_send, h_in, low, g_part, g_send, g_in, low_grad,
    b_part, b_in,
    cot_s, cot_r, ag_s, ag_r, sum_s, sum_r, all_s, all_r,
    cross_s, cross_r, rs_s, rs_r, bias_s, bias_r, local,
):
    me = lax.axis_index("dp")
    mf = lax.axis_index("feat")
    rows, cols = x.shape
    part = rows // n_feat
    rank = u_full.shape[0]
    shard = rank // n_dp
    tiles = cols // TILE
    odd = lax.rem(me, 2)

    def flip(mask):
        return me + mask - 2 * mask * lax.rem(lax.div(me, mask), 2)

    masks = [2 ** (b + 1) for b in range(steps - 1)]
    peers = [
        (1 - odd) * flip(a) + odd * flip(b) for a, b in zip(masks, masks[::-1])
    ] + [flip(1)]
    feats = [lax.rem(mf + k, n_feat) for k in range(1, n_feat)]

    def rows_of(f):
        return pl.ds(pl.multiple_of(f * part, part), part)

    def cols_of(f):
        return pl.ds(pl.multiple_of(f * cols, cols), cols)

    def tile_at(t):
        return pl.ds(pl.multiple_of(t * TILE, TILE), TILE)

    def slots(a, b):
        return pl.ds(a * shard, (b - a) * shard)

    started = []

    def send(src, dst, s, r, dp, feat):
        copy = pltpu.make_async_remote_copy(
            src_ref=src, dst_ref=dst, send_sem=s, recv_sem=r,
            device_id=(dp, feat), device_id_type=MESH,
        )
        copy.start()
        started.append(copy)
        return copy

    def move(src, dst, s):
        copy = pltpu.make_async_copy(src, dst, s)
        copy.start()
        return copy

    barrier = pltpu.get_barrier_semaphore()
    for p in peers:
        pl.semaphore_signal(barrier, inc=1, device_id=(p, mf), device_id_type=MESH)
    for f in feats:
        pl.semaphore_signal(barrier, inc=1, device_id=(me, f), device_id_type=MESH)
    pl.semaphore_wait(barrier, steps + n_feat - 1)

    first = [
        send(src, full.at[slots(1, 2), :], ag_s.at[w, 0], ag_r.at[w, 0], peers[0], mf)
        for w, (src, full) in enumerate(((down, d_full), (up, u_full)))
    ]
    cot_in = [
        send(cot.at[:, cols_of(f)], cot_v.at[rows_of(mf), :], cot_s.at[k], cot_r.at[k], me, f)
        for k, f in enumerate(feats)
    ]
    own = [
        move(down, d_full.at[slots(0, 1), :], local.at[0]),
        move(up, u_full.at[slots(0, 1), :], local.at[1]),
        move(cot.at[:, cols_of(mf)], cot_v.at[rows_of(mf), :], local.at[2]),
    ]

    mid = 2 ** (steps - 1)
    half = mid // 2

    def swap(w, full, s, lo, hi, to, sem):
        return send(
            full.at[slots(lo, hi), :], full.at[slots(to, to + hi - lo), :],
            ag_s.at[w, sem], ag_r.at[w, sem], peers[s], mf)

    hops, early = list(first), [None, None]
    for s in range(1, steps - 1):
        for w, full in enumerate((d_full, u_full)):
            if s == 1:
                own[w].wait()
            hops[w].wait_recv()
            hops[w] = swap(w, full, s, 0, 2 ** s, 2 ** s, s)
            if s == steps - 2:
                early[w] = swap(w, full, steps - 1, 0, half, mid, steps - 1)

    def last_hop(w, full):
        hops[w].wait_recv()
        late = swap(w, full, steps - 1, half, mid, mid + half, steps)
        early[w].wait_recv()
        return late

    def spread_parts(which, total, outgoing, incoming):
        copies = []
        for k, f in enumerate(feats):
            outgoing[rows_of(f), :] = total[rows_of(f), :].astype(BF16)
            copies.append(send(
                outgoing.at[rows_of(f), :], incoming.at[k],
                sum_s.at[which, k], sum_r.at[which, k], me, f))
        return copies

    def share_sum(which, total, incoming, copies, result):
        value = total[rows_of(mf), :]
        for k, copy in enumerate(copies):
            copy.wait_recv()
            value = value + incoming[k].astype(F32)
        result[rows_of(mf), :] = value.astype(BF16)
        return [
            send(result.at[rows_of(mf), :], result.at[rows_of(mf), :],
                 all_s.at[which, k], all_r.at[which, k], me, f)
            for k, f in enumerate(feats)
        ]

    def wait_all(copies):
        for copy in copies:
            copy.wait_recv()

    last_hop(0, d_full).wait_recv()
    h_part[...] = jnp.zeros_like(h_part)

    @pl.loop(0, tiles)
    def _(t):
        c = tile_at(t)
        h_part[...] += lax.dot_general(x[:, c], d_full[:, c], NT, preferred_element_type=F32)

    parts = spread_parts(0, h_part, h_send, h_in)
    u_late = last_hop(1, u_full)
    shares = share_sum(0, h_part, h_in, parts, low)
    u_late.wait_recv()
    wait_all(shares)

    cross_in, own_cross = [], []
    per_chunk = tiles // CHUNKS
    for n in range(CHUNKS):

        @pl.loop(n * per_chunk, (n + 1) * per_chunk)
        def _(t):
            c = tile_at(t)
            proj = jnp.dot(low[...], u_full[:, c], preferred_element_type=F32)
            plus = 1.0 + (gate[...] * proj + bias[:, c])
            one_scale[:, c] = plus
            cross[:, c] = (x[:, c].astype(F32) * plus).astype(BF16)

        width = per_chunk * TILE
        here = pl.ds(n * width, width)
        there = pl.ds(pl.multiple_of(mf * cols + n * width, width), width)
        for k, f in enumerate(feats):
            cross_in.append(send(
                cross.at[rows_of(f), here], cross_out.at[:, there],
                cross_s.at[n, k], cross_r.at[n, k], me, f))
        own_cross.append(move(cross.at[rows_of(mf), here], cross_out.at[:, there], local.at[3 + n]))

    own[2].wait()
    wait_all(cot_in)
    g_part[...] = jnp.zeros_like(g_part)

    @pl.loop(0, tiles)
    def _(t):
        c = tile_at(t)
        pre = cot_v[:, c].astype(F32) * x[:, c].astype(F32)
        b_part[:, c] = jnp.sum(pre.reshape(rows // 8, 8, TILE), axis=0)
        scaled = (gate[...] * pre).astype(BF16)
        gated[:, c] = scaled
        g_part[...] += lax.dot_general(scaled, u_full[:, c], NT, preferred_element_type=F32)

    parts = spread_parts(1, g_part, g_send, g_in)

    def outer(factor, block, acc, out):
        @pl.loop(0, tiles)
        def _(t):
            c = tile_at(t)
            terms = jnp.dot(factor, block[:, c], preferred_element_type=F32)
            acc[:, c] = terms[: mid * shard]
            out[slots(mid, 2 * mid), c] = terms[mid * shard :].astype(BF16)

    def scatter(w, s, out, arriving):
        return send(
            out.at[slots(2 ** s, 2 ** (s + 1)), :], arriving.at[slots(2 ** s, 2 ** (s + 1)), :],
            rs_s.at[w, s], rs_r.at[w, s], peers[s], mf)

    def fold(s, copy, acc, out, arriving, result):
        copy.wait_recv()
        n = 2 ** s

        @pl.loop(0, tiles)
        def _(t):
            c = tile_at(t)
            total = acc[slots(0, n), c] + arriving[slots(n, 2 * n), c].astype(F32)
            if s == 0:
                result[:, c] = total
            else:
                acc[slots(0, n // 2), c] = total[: n // 2 * shard]
                out[slots(n // 2, n), c] = total[n // 2 * shard :].astype(BF16)

    def bias_send(s):
        return send(b_part, b_in.at[s], bias_s.at[s], bias_r.at[s], peers[s], mf)

    def bias_fold(s, copy):
        copy.wait()
        started[:] = [other for other in started if other is not copy]
        b_part[...] += b_in[s]

    ups = (acc_up, out_up, in_up, grad_up)
    downs = (acc_down, out_down, in_down, grad_down)
    bias_hop = bias_send(steps - 1)
    outer(low[...].astype(F32).T.astype(BF16), gated, acc_up, out_up)
    up_hop = scatter(0, steps - 1, out_up, in_up)

    shares = share_sum(1, g_part, g_in, parts, low_grad)
    fold(steps - 1, up_hop, *ups)
    up_hop = scatter(0, steps - 2, out_up, in_up)
    wait_all(shares)

    outer(low_grad[...].astype(F32).T.astype(BF16), x, acc_down, out_down)
    down_hop = scatter(1, steps - 1, out_down, in_down)
    bias_fold(steps - 1, bias_hop)
    bias_hop = bias_send(steps - 2)
    fold(steps - 1, down_hop, *downs)
    down_hop = scatter(1, steps - 2, out_down, in_down)

    @pl.loop(0, tiles)
    def _(t):
        c = tile_at(t)
        back = jnp.dot(low_grad[...], d_full[:, c], preferred_element_type=F32)
        grad_in[:, c] = (cot_v[:, c].astype(F32) * one_scale[:, c] + back).astype(BF16)

    for s in range(steps - 2, -1, -1):
        fold(s, up_hop, *ups)
        if s:
            up_hop = scatter(0, s - 1, out_up, in_up)
        fold(s, down_hop, *downs)
        if s:
            down_hop = scatter(1, s - 1, out_down, in_down)
        bias_fold(s, bias_hop)
        if s:
            bias_hop = bias_send(s - 1)
    grad_bias[...] = jnp.sum(b_part[...], axis=0, keepdims=True)

    wait_all(cross_in)
    for copy in own_cross:
        copy.wait()
    for copy in started:
        copy.wait_send()


def kernel_form(n_dp, n_feat, features, gate, bias, down_weight, up_weight, cotangent):
    rows, cols = features.shape
    shard = up_weight.shape[0]
    rank = shard * n_dp
    part = rows // n_feat
    steps = n_dp.bit_length() - 1
    vmem = pl.BlockSpec(memory_space=pltpu.VMEM)
    hbm = pl.BlockSpec(memory_space=pl.ANY)
    dma = pltpu.SemaphoreType.DMA
    others = n_feat - 1
    cross_out, grad_up, grad_down, grad_bias, grad_in = pl.pallas_call(
        functools.partial(kernel, n_dp, n_feat, steps),
        out_shape=(
            jax.ShapeDtypeStruct((part, cols * n_feat), BF16),
            jax.ShapeDtypeStruct((shard, cols), F32),
            jax.ShapeDtypeStruct((shard, cols), F32),
            jax.ShapeDtypeStruct((1, cols), F32),
            jax.ShapeDtypeStruct((rows, cols), BF16),
        ),
        in_specs=[vmem, hbm, hbm, hbm, vmem, vmem],
        out_specs=(hbm, vmem, vmem, vmem, vmem),
        scratch_shapes=[
            pltpu.VMEM((rows, cols), BF16),
            pltpu.VMEM((rank, cols), BF16),
            pltpu.VMEM((rank, cols), BF16),
            pltpu.VMEM((rows, cols), F32),
            pltpu.VMEM((rows, cols), BF16),
            pltpu.VMEM((rows, cols), BF16),
            pltpu.VMEM((rank // 2, cols), F32),
            pltpu.VMEM((rank // 2, cols), F32),
            pltpu.VMEM((rank, cols), BF16),
            pltpu.VMEM((rank, cols), BF16),
            pltpu.VMEM((rank, cols), BF16),
            pltpu.VMEM((rank, cols), BF16),
            pltpu.VMEM((rows, rank), F32),
            pltpu.VMEM((rows, rank), BF16),
            pltpu.VMEM((others, part, rank), BF16),
            pltpu.VMEM((rows, rank), BF16),
            pltpu.VMEM((rows, rank), F32),
            pltpu.VMEM((rows, rank), BF16),
            pltpu.VMEM((others, part, rank), BF16),
            pltpu.VMEM((rows, rank), BF16),
            pltpu.VMEM((8, cols), F32),
            pltpu.VMEM((steps, 8, cols), F32),
            dma((others,)), dma((others,)),
            dma((2, steps + 1)), dma((2, steps + 1)),
            dma((2, others)), dma((2, others)),
            dma((2, others)), dma((2, others)),
            dma((CHUNKS, others)), dma((CHUNKS, others)),
            dma((2, steps)), dma((2, steps)),
            dma((steps,)), dma((steps,)),
            dma((3 + CHUNKS,)),
        ],
        compiler_params=pltpu.CompilerParams(
            collective_id=0, has_side_effects=True, vmem_limit_bytes=62 * 2 ** 20
        ),
        cost_estimate=pl.CostEstimate(
            flops=12 * rows * rank * cols, bytes_accessed=16 * rows * cols, transcendentals=0
        ),
    )(features, cotangent, down_weight.T, up_weight, gate[:, None], bias[None, :])
    return cross_out, grad_up, grad_down.T, grad_bias[0], grad_in


def solution(mesh):
    n_dp, n_feat = mesh.shape["dp"], mesh.shape["feat"]

    def on_device(features, gate, bias, down_weight, up_weight, cotangent):
        rows, cols = features.shape
        fits = (
            n_dp >= 4
            and n_dp & (n_dp - 1) == 0
            and n_feat > 1
            and up_weight.shape[0] % 16 == 0
            and rows % (16 * n_feat) == 0
            and cols % (TILE * CHUNKS) == 0
        )
        args = (features, gate, bias, down_weight, up_weight, cotangent)
        return kernel_form(n_dp, n_feat, *args) if fits else plain_form(*args)

    in_specs = (
        P("dp", "feat"),
        P("dp"),
        P("feat"),
        P("feat", "dp"),
        P("dp", "feat"),
        P(("dp", "feat"), None),
    )
    out_specs = (
        P(("dp", "feat"), None),
        P("dp", "feat"),
        P("feat", "dp"),
        P("feat"),
        P("dp", "feat"),
    )
    return jax.shard_map(
        on_device, mesh=mesh, in_specs=in_specs, out_specs=out_specs, check_vma=False
    )
```

```python
import functools

import jax
import jax.numpy as jnp
from jax import lax
from jax.experimental import pallas as pl
from jax.experimental.pallas import tpu as pltpu
from jax.sharding import PartitionSpec as P

MESH = pl.DeviceIdType.MESH
F32 = jnp.float32
BF16 = jnp.bfloat16
NT = (((1,), (1,)), ((), ()))
TILE = 512


def rank_total(partial_value):
    return lax.psum(partial_value, "feat").astype(jnp.bfloat16)


def plain_form(features, gate, bias, down_weight, up_weight, cotangent):
    down_full, up_full = (
        lax.all_gather(down_weight, "dp", axis=1, tiled=True),
        lax.all_gather(up_weight, "dp", axis=0, tiled=True),
    )
    low = rank_total(jnp.dot(features, down_full, preferred_element_type=jnp.float32))
    proj = jnp.dot(low, up_full, preferred_element_type=jnp.float32)
    scale = gate[:, None] * proj + bias[None, :]
    xfloat = features.astype(jnp.float32)
    cross = (xfloat * (1.0 + scale)).astype(jnp.bfloat16)
    cross_out = lax.all_to_all(cross, "feat", split_axis=0, concat_axis=1, tiled=True)
    upstream = lax.all_to_all(cotangent, "feat", split_axis=1, concat_axis=0, tiled=True).astype(
        jnp.float32
    )
    pre_grad = upstream * xfloat
    bias_terms = jnp.sum(pre_grad, axis=0)
    gated_grad = (gate[:, None] * pre_grad).astype(jnp.bfloat16)
    contract_first = (((0,), (0,)), ((), ()))
    rank_grad = lax.dot_general(gated_grad, up_full, NT, preferred_element_type=jnp.float32)
    low_grad = rank_total(rank_grad)
    grad_up = lax.psum_scatter(
        lax.dot_general(low, gated_grad, contract_first, preferred_element_type=jnp.float32),
        "dp",
        scatter_dimension=0,
        tiled=True,
    )
    down_terms = lax.dot_general(
        features, low_grad, contract_first, preferred_element_type=jnp.float32
    )
    grad_down = lax.psum_scatter(down_terms, "dp", scatter_dimension=1, tiled=True)
    grad_bias = lax.psum(bias_terms, "dp")
    back = lax.dot_general(low_grad, down_full, NT, preferred_element_type=jnp.float32)
    grad_in = (upstream * (1.0 + scale) + back).astype(jnp.bfloat16)
    return (cross_out, grad_up, grad_down, grad_bias, grad_in)


def kernel(
    n_dp, n_feat, steps,
    x, cot, down, up, gate, bias,
    cross_out, grad_up, grad_down, grad_bias, grad_in,
    cot_v, d_full, u_full, one_scale, cross,
    low_t, acc_up, acc_down, out_up, out_down, in_up, in_down,
    gate_v, h_part, h_send, h_in, low, g_part, g_send, g_in, low_grad,
    b_part, b_in,
    cot_s, cot_r, ag_s, ag_r, sum_s, sum_r, all_s, all_r,
    cross_s, cross_r, rs_s, rs_r, bias_s, bias_r, local,
):
    me = lax.axis_index("dp")
    mf = lax.axis_index("feat")
    rows, cols = x.shape
    part = rows // n_feat
    rank = u_full.shape[0]
    shard = rank // n_dp
    tiles = cols // TILE
    odd = lax.rem(me, 2)

    def flip(mask):
        return me + mask - 2 * mask * lax.rem(lax.div(me, mask), 2)

    masks = [2 ** (b + 1) for b in range(steps - 1)]
    peers = [
        (1 - odd) * flip(a) + odd * flip(b) for a, b in zip(masks, masks[::-1])
    ] + [flip(1)]
    feats = [lax.rem(mf + k, n_feat) for k in range(1, n_feat)]

    def rows_of(f):
        return pl.ds(pl.multiple_of(f * part, part), part)

    def cols_of(f):
        return pl.ds(pl.multiple_of(f * cols, cols), cols)

    def tile_at(t):
        return pl.ds(pl.multiple_of(t * TILE, TILE), TILE)

    def slots(a, b):
        return pl.ds(a * shard, (b - a) * shard)

    started = []

    def send(src, dst, s, r, dp, feat):
        copy = pltpu.make_async_remote_copy(
            src_ref=src, dst_ref=dst, send_sem=s, recv_sem=r,
            device_id=(dp, feat), device_id_type=MESH,
        )
        copy.start()
        started.append(copy)
        return copy

    def move(src, dst, s):
        copy = pltpu.make_async_copy(src, dst, s)
        copy.start()
        return copy

    def cot_copy(t, k, f):
        there = pl.ds(pl.multiple_of(f * cols + t * TILE, TILE), TILE)
        return pltpu.make_async_remote_copy(
            src_ref=cot.at[:, there], dst_ref=cot_v.at[rows_of(mf), tile_at(t)],
            send_sem=cot_s.at[t, k], recv_sem=cot_r.at[t, k],
            device_id=(me, f), device_id_type=MESH,
        )

    def cross_copy(t, k, f):
        there = pl.ds(pl.multiple_of(mf * cols + t * TILE, TILE), TILE)
        return pltpu.make_async_remote_copy(
            src_ref=cross.at[rows_of(f), tile_at(t)], dst_ref=cross_out.at[:, there],
            send_sem=cross_s.at[t, k], recv_sem=cross_r.at[t, k],
            device_id=(me, f), device_id_type=MESH,
        )

    def start_chunks(copy_of, lo, hi):
        @pl.loop(lo, hi)
        def _(t):
            for k, f in enumerate(feats):
                copy_of(t, k, f).start()

    barrier = pltpu.get_barrier_semaphore()
    for p in peers:
        pl.semaphore_signal(barrier, inc=1, device_id=(p, mf), device_id_type=MESH)
    for f in feats:
        pl.semaphore_signal(barrier, inc=1, device_id=(me, f), device_id_type=MESH)
    own = [
        move(down, d_full.at[slots(0, 1), :], local.at[0]),
        move(up, u_full.at[slots(0, 1), :], local.at[1]),
        move(cot.at[:, cols_of(mf)], cot_v.at[rows_of(mf), :], local.at[2]),
    ]
    gate_v[...] = jnp.broadcast_to(gate[...], (128, rows)).T
    pl.semaphore_wait(barrier, steps + n_feat - 1)

    mid = 2 ** (steps - 1)
    half = mid // 2

    def swap(w, full, s, lo, hi, to, sem):
        return send(
            full.at[slots(lo, hi), :], full.at[slots(to, to + hi - lo), :],
            ag_s.at[w, sem], ag_r.at[w, sem], peers[s], mf)

    early = [None, None]

    def first_hop(w, src, full):
        return send(src, full.at[slots(1, 2), :], ag_s.at[w, 0], ag_r.at[w, 0], peers[0], mf)

    def middle_hops(w, full, hop):
        own[w].wait()
        for s in range(1, steps - 1):
            hop.wait_recv()
            hop = swap(w, full, s, 0, 2 ** s, 2 ** s, s)
            if s == steps - 2:
                early[w] = swap(w, full, steps - 1, 0, half, mid, steps - 1)
        return hop

    def last_hop(w, full, hop):
        hop.wait_recv()
        return swap(w, full, steps - 1, half, mid, mid + half, steps)

    def spread_parts(which, total, outgoing, incoming):
        copies = []
        for k, f in enumerate(feats):
            outgoing[rows_of(f), :] = total[rows_of(f), :].astype(BF16)
            copies.append(send(
                outgoing.at[rows_of(f), :], incoming.at[k],
                sum_s.at[which, k], sum_r.at[which, k], me, f))
        return copies

    def share_sum(which, total, incoming, copies, result):
        value = total[rows_of(mf), :]
        for k, copy in enumerate(copies):
            copy.wait_recv()
            value = value + incoming[k].astype(F32)
        result[rows_of(mf), :] = value.astype(BF16)
        return [
            send(result.at[rows_of(mf), :], result.at[rows_of(mf), :],
                 all_s.at[which, k], all_r.at[which, k], me, f)
            for k, f in enumerate(feats)
        ]

    def wait_all(copies):
        for copy in copies:
            copy.wait_recv()

    def bias_send(s):
        return send(b_part, b_in.at[s], bias_s.at[s], bias_r.at[s], peers[s], mf)

    def bias_fold(s, copy):
        copy.wait()
        started[:] = [other for other in started if other is not copy]
        b_part[...] += b_in[s]

    hop = first_hop(0, down, d_full)
    start_chunks(cot_copy, 0, tiles // 2)
    hop = middle_hops(0, d_full, hop)
    late = last_hop(0, d_full, hop)
    hop = first_hop(1, up, u_full)
    near, far = slots(0, mid), slots(mid, 2 * mid)
    h_part[:, near] = lax.dot_general(x[...], d_full[near, :], NT, preferred_element_type=F32)
    early[0].wait_recv()
    late.wait_recv()
    h_part[:, far] = lax.dot_general(x[...], d_full[far, :], NT, preferred_element_type=F32)
    parts = spread_parts(0, h_part, h_send, h_in)
    start_chunks(cot_copy, tiles // 2, tiles // 2 + 1)
    hop = middle_hops(1, u_full, hop)
    shares = share_sum(0, h_part, h_in, parts, low)
    start_chunks(cot_copy, tiles // 2 + 1, tiles)
    late = last_hop(1, u_full, hop)
    wait_all(shares)
    early[1].wait_recv()
    late.wait_recv()

    @pl.loop(0, tiles)
    def _(t):
        c = tile_at(t)
        proj = jnp.dot(low[...], u_full[:, c], preferred_element_type=F32)
        plus = 1.0 + (gate_v[:, :1] * proj + bias[:, c])
        one_scale[:, c] = plus
        cross[:, c] = (x[:, c].astype(F32) * plus).astype(BF16)

    start_chunks(cross_copy, 0, tiles // 4)
    own_cross = move(cross.at[rows_of(mf), :], cross_out.at[:, cols_of(mf)], local.at[3])

    own[2].wait()
    g_part[...] = jnp.zeros_like(g_part)
    low_t[...] = low[...].astype(F32).T.astype(BF16)

    @pl.loop(0, tiles)
    def _(t):
        c = tile_at(t)
        for k, f in enumerate(feats):
            cot_copy(t, k, f).wait_recv()
        pre = cot_v[:, c].astype(F32) * x[:, c].astype(F32)
        b_part[:, c] = jnp.sum(pre.reshape(rows // 8, 8, TILE), axis=0)
        scaled = (gate_v[:, :1] * pre).astype(BF16)
        g_part[...] += lax.dot_general(scaled, u_full[:, c], NT, preferred_element_type=F32)
        terms = jnp.dot(low_t[...], scaled, preferred_element_type=F32)
        acc_up[:, c] = terms[: mid * shard]
        out_up[far, c] = terms[mid * shard :].astype(BF16)

    parts = spread_parts(1, g_part, g_send, g_in)
    start_chunks(cross_copy, tiles // 4, tiles // 2)

    def scatter(w, s, out, arriving):
        return send(
            out.at[slots(2 ** s, 2 ** (s + 1)), :], arriving.at[slots(2 ** s, 2 ** (s + 1)), :],
            rs_s.at[w, s], rs_r.at[w, s], peers[s], mf)

    def fold(s, copy, acc, out, arriving, result):
        copy.wait_recv()
        n = 2 ** s

        @pl.loop(0, tiles)
        def _(t):
            c = tile_at(t)
            total = acc[slots(0, n), c] + arriving[slots(n, 2 * n), c].astype(F32)
            if s == 0:
                result[:, c] = total
            else:
                acc[slots(0, n // 2), c] = total[: n // 2 * shard]
                out[slots(n // 2, n), c] = total[n // 2 * shard :].astype(BF16)

    ups = (acc_up, out_up, in_up, grad_up)
    downs = (acc_down, out_down, in_down, grad_down)
    bias_hop = bias_send(steps - 1)
    up_hop = scatter(0, steps - 1, out_up, in_up)

    shares = share_sum(1, g_part, g_in, parts, low_grad)
    start_chunks(cross_copy, tiles // 2, tiles)
    fold(steps - 1, up_hop, *ups)
    up_hop = scatter(0, steps - 2, out_up, in_up)
    wait_all(shares)
    low_t[...] = low_grad[...].astype(F32).T.astype(BF16)

    @pl.loop(0, tiles)
    def _(t):
        c = tile_at(t)
        terms = jnp.dot(low_t[...], x[:, c], preferred_element_type=F32)
        acc_down[:, c] = terms[: mid * shard]
        out_down[far, c] = terms[mid * shard :].astype(BF16)

    down_hop = scatter(1, steps - 1, out_down, in_down)
    bias_fold(steps - 1, bias_hop)
    bias_hop = bias_send(steps - 2)
    fold(steps - 1, down_hop, *downs)
    down_hop = scatter(1, steps - 2, out_down, in_down)

    @pl.loop(0, tiles)
    def _(t):
        c = tile_at(t)
        back = jnp.dot(low_grad[...], d_full[:, c], preferred_element_type=F32)
        grad_in[:, c] = (cot_v[:, c].astype(F32) * one_scale[:, c] + back).astype(BF16)

    for s in range(steps - 2, -1, -1):
        fold(s, up_hop, *ups)
        if s:
            up_hop = scatter(0, s - 1, out_up, in_up)
        fold(s, down_hop, *downs)
        if s:
            down_hop = scatter(1, s - 1, out_down, in_down)
        bias_fold(s, bias_hop)
        if s:
            bias_hop = bias_send(s - 1)
    grad_bias[...] = jnp.sum(b_part[...], axis=0, keepdims=True)

    @pl.loop(0, tiles)
    def _(t):
        for k, f in enumerate(feats):
            cross_copy(t, k, f).wait_recv()
            cross_copy(t, k, f).wait_send()
            cot_copy(t, k, f).wait_send()

    own_cross.wait()
    for copy in started:
        copy.wait_send()


def kernel_form(n_dp, n_feat, features, gate, bias, down_weight, up_weight, cotangent):
    rows, cols = features.shape
    shard = up_weight.shape[0]
    rank = shard * n_dp
    part = rows // n_feat
    steps = n_dp.bit_length() - 1
    vmem = pl.BlockSpec(memory_space=pltpu.VMEM)
    hbm = pl.BlockSpec(memory_space=pl.ANY)
    dma = pltpu.SemaphoreType.DMA
    others = n_feat - 1
    tiles = cols // TILE
    cross_out, grad_up, grad_down, grad_bias, grad_in = pl.pallas_call(
        functools.partial(kernel, n_dp, n_feat, steps),
        out_shape=(
            jax.ShapeDtypeStruct((part, cols * n_feat), BF16),
            jax.ShapeDtypeStruct((shard, cols), F32),
            jax.ShapeDtypeStruct((shard, cols), F32),
            jax.ShapeDtypeStruct((1, cols), F32),
            jax.ShapeDtypeStruct((rows, cols), BF16),
        ),
        in_specs=[vmem, hbm, hbm, hbm, vmem, vmem],
        out_specs=(hbm, vmem, vmem, vmem, vmem),
        scratch_shapes=[
            pltpu.VMEM((rows, cols), BF16),
            pltpu.VMEM((rank, cols), BF16),
            pltpu.VMEM((rank, cols), BF16),
            pltpu.VMEM((rows, cols), F32),
            pltpu.VMEM((rows, cols), BF16),
            pltpu.VMEM((rank, rows), BF16),
            pltpu.VMEM((rank // 2, cols), F32),
            pltpu.VMEM((rank // 2, cols), F32),
            pltpu.VMEM((rank, cols), BF16),
            pltpu.VMEM((rank, cols), BF16),
            pltpu.VMEM((rank, cols), BF16),
            pltpu.VMEM((rank, cols), BF16),
            pltpu.VMEM((rows, 128), F32),
            pltpu.VMEM((rows, rank), F32),
            pltpu.VMEM((rows, rank), BF16),
            pltpu.VMEM((others, part, rank), BF16),
            pltpu.VMEM((rows, rank), BF16),
            pltpu.VMEM((rows, rank), F32),
            pltpu.VMEM((rows, rank), BF16),
            pltpu.VMEM((others, part, rank), BF16),
            pltpu.VMEM((rows, rank), BF16),
            pltpu.VMEM((8, cols), F32),
            pltpu.VMEM((steps, 8, cols), F32),
            dma((tiles, others)), dma((tiles, others)),
            dma((2, steps + 1)), dma((2, steps + 1)),
            dma((2, others)), dma((2, others)),
            dma((2, others)), dma((2, others)),
            dma((tiles, others)), dma((tiles, others)),
            dma((2, steps)), dma((2, steps)),
            dma((steps,)), dma((steps,)),
            dma((4,)),
        ],
        compiler_params=pltpu.CompilerParams(
            collective_id=0, has_side_effects=True, vmem_limit_bytes=62 * 2 ** 20
        ),
        cost_estimate=pl.CostEstimate(
            flops=12 * rows * rank * cols, bytes_accessed=16 * rows * cols, transcendentals=0
        ),
    )(features, cotangent, down_weight.T, up_weight, gate[None, :], bias[None, :])
    return cross_out, grad_up, grad_down.T, grad_bias[0], grad_in


def solution(mesh):
    n_dp, n_feat = mesh.shape["dp"], mesh.shape["feat"]

    def on_device(features, gate, bias, down_weight, up_weight, cotangent):
        rows, cols = features.shape
        fits = (
            n_dp >= 4
            and n_dp & (n_dp - 1) == 0
            and n_feat > 1
            and up_weight.shape[0] % 16 == 0
            and rows % (16 * n_feat) == 0
            and cols % TILE == 0 and cols // TILE >= 8
        )
        args = (features, gate, bias, down_weight, up_weight, cotangent)
        return kernel_form(n_dp, n_feat, *args) if fits else plain_form(*args)

    in_specs = (
        P("dp", "feat"),
        P("dp"),
        P("feat"),
        P("feat", "dp"),
        P("dp", "feat"),
        P(("dp", "feat"), None),
    )
    out_specs = (
        P(("dp", "feat"), None),
        P("dp", "feat"),
        P("feat", "dp"),
        P("feat"),
        P("dp", "feat"),
    )
    return jax.shard_map(
        on_device, mesh=mesh, in_specs=in_specs, out_specs=out_specs, check_vma=False
    )
```

```python
import functools

import jax
import jax.numpy as jnp
from jax import lax
from jax.experimental import pallas as pl
from jax.experimental.pallas import tpu as pltpu
from jax.sharding import PartitionSpec as P

MESH = pl.DeviceIdType.MESH
F32 = jnp.float32
BF16 = jnp.bfloat16
NT = (((1,), (1,)), ((), ()))
TILE = 512


def rank_total(partial_value):
    return lax.psum(partial_value, "feat").astype(jnp.bfloat16)


def plain_form(features, gate, bias, down_weight, up_weight, cotangent):
    down_full, up_full = (
        lax.all_gather(down_weight, "dp", axis=1, tiled=True),
        lax.all_gather(up_weight, "dp", axis=0, tiled=True),
    )
    low = rank_total(jnp.dot(features, down_full, preferred_element_type=jnp.float32))
    proj = jnp.dot(low, up_full, preferred_element_type=jnp.float32)
    scale = gate[:, None] * proj + bias[None, :]
    xfloat = features.astype(jnp.float32)
    cross = (xfloat * (1.0 + scale)).astype(jnp.bfloat16)
    cross_out = lax.all_to_all(cross, "feat", split_axis=0, concat_axis=1, tiled=True)
    upstream = lax.all_to_all(cotangent, "feat", split_axis=1, concat_axis=0, tiled=True).astype(
        jnp.float32
    )
    pre_grad = upstream * xfloat
    bias_terms = jnp.sum(pre_grad, axis=0)
    gated_grad = (gate[:, None] * pre_grad).astype(jnp.bfloat16)
    contract_first = (((0,), (0,)), ((), ()))
    rank_grad = lax.dot_general(gated_grad, up_full, NT, preferred_element_type=jnp.float32)
    low_grad = rank_total(rank_grad)
    grad_up = lax.psum_scatter(
        lax.dot_general(low, gated_grad, contract_first, preferred_element_type=jnp.float32),
        "dp",
        scatter_dimension=0,
        tiled=True,
    )
    down_terms = lax.dot_general(
        features, low_grad, contract_first, preferred_element_type=jnp.float32
    )
    grad_down = lax.psum_scatter(down_terms, "dp", scatter_dimension=1, tiled=True)
    grad_bias = lax.psum(bias_terms, "dp")
    back = lax.dot_general(low_grad, down_full, NT, preferred_element_type=jnp.float32)
    grad_in = (upstream * (1.0 + scale) + back).astype(jnp.bfloat16)
    return (cross_out, grad_up, grad_down, grad_bias, grad_in)


def kernel(
    n_dp, n_feat, steps,
    x, cot, down, up, gate, bias,
    cross_out, grad_up, grad_down, grad_bias, grad_in,
    cot_v, d_full, u_full, one_scale, cross,
    low_t, acc_up, acc_down, out_up, out_down, in_up, in_down,
    gate_v, h_part, h_send, h_in, low, g_part, g_send, g_in, low_grad,
    b_part, b_in,
    cot_s, cot_r, ag_s, ag_r, sum_s, sum_r, all_s, all_r,
    cross_s, cross_r, rs_s, rs_r, bias_s, bias_r, local,
):
    me = lax.axis_index("dp")
    mf = lax.axis_index("feat")
    rows, cols = x.shape
    part = rows // n_feat
    rank = u_full.shape[0]
    shard = rank // n_dp
    tiles = cols // TILE
    odd = lax.rem(me, 2)

    def flip(mask):
        return me + mask - 2 * mask * lax.rem(lax.div(me, mask), 2)

    masks = [2 ** (b + 1) for b in range(steps - 1)]
    peers = [
        (1 - odd) * flip(a) + odd * flip(b) for a, b in zip(masks, masks[::-1])
    ] + [flip(1)]
    feats = [lax.rem(mf + k, n_feat) for k in range(1, n_feat)]

    def rows_of(f):
        return pl.ds(pl.multiple_of(f * part, part), part)

    def cols_of(f):
        return pl.ds(pl.multiple_of(f * cols, cols), cols)

    def tile_at(t):
        return pl.ds(pl.multiple_of(t * TILE, TILE), TILE)

    def slots(a, b):
        return pl.ds(a * shard, (b - a) * shard)

    started = []

    def send(src, dst, s, r, dp, feat):
        copy = pltpu.make_async_remote_copy(
            src_ref=src, dst_ref=dst, send_sem=s, recv_sem=r,
            device_id=(dp, feat), device_id_type=MESH,
        )
        copy.start()
        started.append(copy)
        return copy

    def move(src, dst, s):
        copy = pltpu.make_async_copy(src, dst, s)
        copy.start()
        return copy

    def cot_copy(t, k, f):
        there = pl.ds(pl.multiple_of(f * cols + t * TILE, TILE), TILE)
        return pltpu.make_async_remote_copy(
            src_ref=cot.at[:, there], dst_ref=cot_v.at[rows_of(mf), tile_at(t)],
            send_sem=cot_s.at[t, k], recv_sem=cot_r.at[t, k],
            device_id=(me, f), device_id_type=MESH,
        )

    def cross_copy(t, k, f):
        there = pl.ds(pl.multiple_of(mf * cols + t * TILE, TILE), TILE)
        return pltpu.make_async_remote_copy(
            src_ref=cross.at[rows_of(f), tile_at(t)], dst_ref=cross_out.at[:, there],
            send_sem=cross_s.at[t, k], recv_sem=cross_r.at[t, k],
            device_id=(me, f), device_id_type=MESH,
        )

    def start_chunks(copy_of, lo, hi):
        @pl.loop(lo, hi)
        def _(t):
            for k, f in enumerate(feats):
                copy_of(t, k, f).start()

    barrier = pltpu.get_barrier_semaphore()
    for p in peers:
        pl.semaphore_signal(barrier, inc=1, device_id=(p, mf), device_id_type=MESH)
    for f in feats:
        pl.semaphore_signal(barrier, inc=1, device_id=(me, f), device_id_type=MESH)
    own = [
        move(down, d_full.at[slots(0, 1), :], local.at[0]),
        move(up, u_full.at[slots(0, 1), :], local.at[1]),
        move(cot.at[:, cols_of(mf)], cot_v.at[rows_of(mf), :], local.at[2]),
    ]
    gate_v[...] = jnp.broadcast_to(gate[...], (128, rows)).T
    pl.semaphore_wait(barrier, steps + n_feat - 1)

    mid = 2 ** (steps - 1)
    half = mid // 2

    def swap(w, full, s, lo, hi, to, sem):
        return send(
            full.at[slots(lo, hi), :], full.at[slots(to, to + hi - lo), :],
            ag_s.at[w, sem], ag_r.at[w, sem], peers[s], mf)

    early = [None, None]

    def first_hop(w, src, full):
        return send(src, full.at[slots(1, 2), :], ag_s.at[w, 0], ag_r.at[w, 0], peers[0], mf)

    def middle_hops(w, full, hop):
        own[w].wait()
        for s in range(1, steps - 1):
            hop.wait_recv()
            hop = swap(w, full, s, 0, 2 ** s, 2 ** s, s)
            if s == steps - 2:
                early[w] = swap(w, full, steps - 1, 0, half, mid, steps - 1)
        return hop

    def last_hop(w, full, hop):
        hop.wait_recv()
        return swap(w, full, steps - 1, half, mid, mid + half, steps)

    def spread_parts(which, total, outgoing, incoming):
        copies = []
        for k, f in enumerate(feats):
            outgoing[rows_of(f), :] = total[rows_of(f), :].astype(BF16)
            copies.append(send(
                outgoing.at[rows_of(f), :], incoming.at[k],
                sum_s.at[which, k], sum_r.at[which, k], me, f))
        return copies

    def share_sum(which, total, incoming, copies, result):
        value = total[rows_of(mf), :]
        for k, copy in enumerate(copies):
            copy.wait_recv()
            value = value + incoming[k].astype(F32)
        result[rows_of(mf), :] = value.astype(BF16)
        return [
            send(result.at[rows_of(mf), :], result.at[rows_of(mf), :],
                 all_s.at[which, k], all_r.at[which, k], me, f)
            for k, f in enumerate(feats)
        ]

    def wait_all(copies):
        for copy in copies:
            copy.wait_recv()

    def bias_send(s):
        return send(b_part, b_in.at[s], bias_s.at[s], bias_r.at[s], peers[s], mf)

    def bias_fold(s, copy):
        copy.wait()
        started[:] = [other for other in started if other is not copy]
        b_part[...] += b_in[s]

    hop = first_hop(0, down, d_full)
    start_chunks(cot_copy, 0, tiles * 3 // 4)
    hop = middle_hops(0, d_full, hop)
    late = last_hop(0, d_full, hop)
    hop = first_hop(1, up, u_full)
    near, far = slots(0, mid), slots(mid, 2 * mid)
    h_part[:, near] = lax.dot_general(x[...], d_full[near, :], NT, preferred_element_type=F32)
    early[0].wait_recv()
    late.wait_recv()
    h_part[:, far] = lax.dot_general(x[...], d_full[far, :], NT, preferred_element_type=F32)
    parts = spread_parts(0, h_part, h_send, h_in)
    start_chunks(cot_copy, tiles * 3 // 4, tiles * 7 // 8)
    hop = middle_hops(1, u_full, hop)
    shares = share_sum(0, h_part, h_in, parts, low)
    start_chunks(cot_copy, tiles * 7 // 8, tiles)
    late = last_hop(1, u_full, hop)
    wait_all(shares)
    early[1].wait_recv()
    late.wait_recv()

    @pl.loop(0, tiles)
    def _(t):
        c = tile_at(t)
        proj = jnp.dot(low[...], u_full[:, c], preferred_element_type=F32)
        plus = 1.0 + (gate_v[:, :1] * proj + bias[:, c])
        one_scale[:, c] = plus
        cross[:, c] = (x[:, c].astype(F32) * plus).astype(BF16)

    start_chunks(cross_copy, 0, tiles * 3 // 8)
    own_cross = move(cross.at[rows_of(mf), :], cross_out.at[:, cols_of(mf)], local.at[3])

    own[2].wait()
    g_part[...] = jnp.zeros_like(g_part)
    low_t[...] = low[...].astype(F32).T.astype(BF16)

    @pl.loop(0, tiles)
    def _(t):
        c = tile_at(t)
        for k, f in enumerate(feats):
            cot_copy(t, k, f).wait_recv()
        pre = cot_v[:, c].astype(F32) * x[:, c].astype(F32)
        b_part[:, c] = jnp.sum(pre.reshape(rows // 8, 8, TILE), axis=0)
        scaled = (gate_v[:, :1] * pre).astype(BF16)
        g_part[...] += lax.dot_general(scaled, u_full[:, c], NT, preferred_element_type=F32)
        terms = jnp.dot(low_t[...], scaled, preferred_element_type=F32)
        acc_up[:, c] = terms[: mid * shard]
        out_up[far, c] = terms[mid * shard :].astype(BF16)

    parts = spread_parts(1, g_part, g_send, g_in)
    start_chunks(cross_copy, tiles * 3 // 8, tiles * 5 // 8)

    def scatter(w, s, out, arriving):
        return send(
            out.at[slots(2 ** s, 2 ** (s + 1)), :], arriving.at[slots(2 ** s, 2 ** (s + 1)), :],
            rs_s.at[w, s], rs_r.at[w, s], peers[s], mf)

    def fold(s, copy, acc, out, arriving, result):
        copy.wait_recv()
        n = 2 ** s

        @pl.loop(0, tiles)
        def _(t):
            c = tile_at(t)
            total = acc[slots(0, n), c] + arriving[slots(n, 2 * n), c].astype(F32)
            if s == 0:
                result[:, c] = total
            else:
                acc[slots(0, n // 2), c] = total[: n // 2 * shard]
                out[slots(n // 2, n), c] = total[n // 2 * shard :].astype(BF16)

    ups = (acc_up, out_up, in_up, grad_up)
    downs = (acc_down, out_down, in_down, grad_down)
    bias_hop = bias_send(steps - 1)
    up_hop = scatter(0, steps - 1, out_up, in_up)

    shares = share_sum(1, g_part, g_in, parts, low_grad)
    start_chunks(cross_copy, tiles * 5 // 8, tiles)
    fold(steps - 1, up_hop, *ups)
    up_hop = scatter(0, steps - 2, out_up, in_up)
    wait_all(shares)
    low_t[...] = low_grad[...].astype(F32).T.astype(BF16)

    @pl.loop(0, tiles)
    def _(t):
        c = tile_at(t)
        terms = jnp.dot(low_t[...], x[:, c], preferred_element_type=F32)
        acc_down[:, c] = terms[: mid * shard]
        out_down[far, c] = terms[mid * shard :].astype(BF16)

    down_hop = scatter(1, steps - 1, out_down, in_down)
    bias_fold(steps - 1, bias_hop)
    bias_hop = bias_send(steps - 2)
    fold(steps - 1, down_hop, *downs)
    down_hop = scatter(1, steps - 2, out_down, in_down)

    @pl.loop(0, tiles)
    def _(t):
        c = tile_at(t)
        back = jnp.dot(low_grad[...], d_full[:, c], preferred_element_type=F32)
        grad_in[:, c] = (cot_v[:, c].astype(F32) * one_scale[:, c] + back).astype(BF16)

    for s in range(steps - 2, -1, -1):
        fold(s, up_hop, *ups)
        if s:
            up_hop = scatter(0, s - 1, out_up, in_up)
        fold(s, down_hop, *downs)
        if s:
            down_hop = scatter(1, s - 1, out_down, in_down)
        bias_fold(s, bias_hop)
        if s:
            bias_hop = bias_send(s - 1)
    grad_bias[...] = jnp.sum(b_part[...], axis=0, keepdims=True)

    @pl.loop(0, tiles)
    def _(t):
        for k, f in enumerate(feats):
            cross_copy(t, k, f).wait_recv()
            cross_copy(t, k, f).wait_send()
            cot_copy(t, k, f).wait_send()

    own_cross.wait()
    for copy in started:
        copy.wait_send()


def hand_over(*refs):
    count = len(refs) // 2
    sems = refs[-1]
    copies = []
    for src, dst in zip(refs[:count], refs[count:-1]):
        rows = src.shape[0]
        pieces = 4 if rows % 64 == 0 else 1
        for n in range(pieces):
            at = pl.ds(n * (rows // pieces), rows // pieces)
            copy = pltpu.make_async_copy(src.at[at, :], dst.at[at, :], sems.at[len(copies)])
            copy.start()
            copies.append(copy)
    for copy in copies:
        copy.wait()


def placed(*values):
    anywhere = [pl.BlockSpec(memory_space=pl.ANY)] * len(values)
    return pl.pallas_call(
        hand_over,
        out_shape=tuple(jax.ShapeDtypeStruct(v.shape, v.dtype) for v in values),
        in_specs=anywhere,
        out_specs=tuple(anywhere),
        scratch_shapes=[pltpu.SemaphoreType.DMA((4 * len(values),))],
        compiler_params=pltpu.CompilerParams(vmem_limit_bytes=62 * 2 ** 20),
    )(*values)


def kernel_form(n_dp, n_feat, features, gate, bias, down_weight, up_weight, cotangent):
    rows, cols = features.shape
    shard = up_weight.shape[0]
    rank = shard * n_dp
    part = rows // n_feat
    steps = n_dp.bit_length() - 1
    vmem = pl.BlockSpec(memory_space=pltpu.VMEM)
    hbm = pl.BlockSpec(memory_space=pl.ANY)
    dma = pltpu.SemaphoreType.DMA
    others = n_feat - 1
    tiles = cols // TILE
    results = pl.pallas_call(
        functools.partial(kernel, n_dp, n_feat, steps),
        out_shape=(
            jax.ShapeDtypeStruct((part, cols * n_feat), BF16),
            jax.ShapeDtypeStruct((shard, cols), F32),
            jax.ShapeDtypeStruct((shard, cols), F32),
            jax.ShapeDtypeStruct((1, cols), F32),
            jax.ShapeDtypeStruct((rows, cols), BF16),
        ),
        in_specs=[vmem, hbm, hbm, hbm, vmem, vmem],
        out_specs=(hbm, vmem, vmem, vmem, vmem),
        scratch_shapes=[
            pltpu.VMEM((rows, cols), BF16),
            pltpu.VMEM((rank, cols), BF16),
            pltpu.VMEM((rank, cols), BF16),
            pltpu.VMEM((rows, cols), F32),
            pltpu.VMEM((rows, cols), BF16),
            pltpu.VMEM((rank, rows), BF16),
            pltpu.VMEM((rank // 2, cols), F32),
            pltpu.VMEM((rank // 2, cols), F32),
            pltpu.VMEM((rank, cols), BF16),
            pltpu.VMEM((rank, cols), BF16),
            pltpu.VMEM((rank, cols), BF16),
            pltpu.VMEM((rank, cols), BF16),
            pltpu.VMEM((rows, 128), F32),
            pltpu.VMEM((rows, rank), F32),
            pltpu.VMEM((rows, rank), BF16),
            pltpu.VMEM((others, part, rank), BF16),
            pltpu.VMEM((rows, rank), BF16),
            pltpu.VMEM((rows, rank), F32),
            pltpu.VMEM((rows, rank), BF16),
            pltpu.VMEM((others, part, rank), BF16),
            pltpu.VMEM((rows, rank), BF16),
            pltpu.VMEM((8, cols), F32),
            pltpu.VMEM((steps, 8, cols), F32),
            dma((tiles, others)), dma((tiles, others)),
            dma((2, steps + 1)), dma((2, steps + 1)),
            dma((2, others)), dma((2, others)),
            dma((2, others)), dma((2, others)),
            dma((tiles, others)), dma((tiles, others)),
            dma((2, steps)), dma((2, steps)),
            dma((steps,)), dma((steps,)),
            dma((4,)),
        ],
        compiler_params=pltpu.CompilerParams(
            collective_id=0, has_side_effects=True, vmem_limit_bytes=62 * 2 ** 20
        ),
        cost_estimate=pl.CostEstimate(
            flops=12 * rows * rank * cols, bytes_accessed=16 * rows * cols, transcendentals=0
        ),
    )(features, cotangent, down_weight.T, up_weight, gate[None, :], bias[None, :])
    cross_out, grad_up, grad_down, grad_bias, grad_in = placed(*results)
    return cross_out, grad_up, grad_down.T, grad_bias[0], grad_in


def solution(mesh):
    n_dp, n_feat = mesh.shape["dp"], mesh.shape["feat"]

    def on_device(features, gate, bias, down_weight, up_weight, cotangent):
        rows, cols = features.shape
        fits = (
            n_dp >= 4
            and n_dp & (n_dp - 1) == 0
            and n_feat > 1
            and up_weight.shape[0] % 16 == 0
            and rows % (16 * n_feat) == 0
            and cols % TILE == 0 and cols // TILE >= 8
        )
        args = (features, gate, bias, down_weight, up_weight, cotangent)
        return kernel_form(n_dp, n_feat, *args) if fits else plain_form(*args)

    in_specs = (
        P("dp", "feat"),
        P("dp"),
        P("feat"),
        P("feat", "dp"),
        P("dp", "feat"),
        P(("dp", "feat"), None),
    )
    out_specs = (
        P(("dp", "feat"), None),
        P("dp", "feat"),
        P("feat", "dp"),
        P("feat"),
        P("dp", "feat"),
    )
    return jax.shard_map(
        on_device, mesh=mesh, in_specs=in_specs, out_specs=out_specs, check_vma=False
    )
```

```python
import functools

import jax
import jax.numpy as jnp
from jax import lax
from jax.experimental import pallas as pl
from jax.experimental.pallas import tpu as pltpu
from jax.sharding import PartitionSpec as P

MESH = pl.DeviceIdType.MESH
F32 = jnp.float32
BF16 = jnp.bfloat16
NT = (((1,), (1,)), ((), ()))
TILE = 512


def rank_total(partial_value):
    return lax.psum(partial_value, "feat").astype(jnp.bfloat16)


def plain_form(features, gate, bias, down_weight, up_weight, cotangent):
    down_full, up_full = (
        lax.all_gather(down_weight, "dp", axis=1, tiled=True),
        lax.all_gather(up_weight, "dp", axis=0, tiled=True),
    )
    low = rank_total(jnp.dot(features, down_full, preferred_element_type=jnp.float32))
    proj = jnp.dot(low, up_full, preferred_element_type=jnp.float32)
    scale = gate[:, None] * proj + bias[None, :]
    xfloat = features.astype(jnp.float32)
    cross = (xfloat * (1.0 + scale)).astype(jnp.bfloat16)
    cross_out = lax.all_to_all(cross, "feat", split_axis=0, concat_axis=1, tiled=True)
    upstream = lax.all_to_all(cotangent, "feat", split_axis=1, concat_axis=0, tiled=True).astype(
        jnp.float32
    )
    pre_grad = upstream * xfloat
    bias_terms = jnp.sum(pre_grad, axis=0)
    gated_grad = (gate[:, None] * pre_grad).astype(jnp.bfloat16)
    contract_first = (((0,), (0,)), ((), ()))
    rank_grad = lax.dot_general(gated_grad, up_full, NT, preferred_element_type=jnp.float32)
    low_grad = rank_total(rank_grad)
    grad_up = lax.psum_scatter(
        lax.dot_general(low, gated_grad, contract_first, preferred_element_type=jnp.float32),
        "dp",
        scatter_dimension=0,
        tiled=True,
    )
    down_terms = lax.dot_general(
        features, low_grad, contract_first, preferred_element_type=jnp.float32
    )
    grad_down = lax.psum_scatter(down_terms, "dp", scatter_dimension=1, tiled=True)
    grad_bias = lax.psum(bias_terms, "dp")
    back = lax.dot_general(low_grad, down_full, NT, preferred_element_type=jnp.float32)
    grad_in = (upstream * (1.0 + scale) + back).astype(jnp.bfloat16)
    return (cross_out, grad_up, grad_down, grad_bias, grad_in)


def kernel(
    n_dp, n_feat, steps,
    x, cot, down, up, gate, bias,
    cross_out, grad_up, grad_down, grad_bias, grad_in,
    cot_own, cot_v, d_full, u_full, one_scale, cross,
    low_t, acc_up, acc_down, out_up, out_down, in_up, in_down,
    gate_v, h_part, h_send, h_in, low, g_part, g_send, g_in, low_grad,
    b_part, b_in,
    cot_s, cot_r, ag_s, ag_r, sum_s, sum_r, all_s, all_r,
    cross_s, cross_r, rs_s, rs_r, bias_s, bias_r, local,
):
    me = lax.axis_index("dp")
    mf = lax.axis_index("feat")
    rows, cols = x.shape
    part = rows // n_feat
    rank = u_full.shape[0]
    shard = rank // n_dp
    tiles = cols // TILE
    odd = lax.rem(me, 2)

    def flip(mask):
        return me + mask - 2 * mask * lax.rem(lax.div(me, mask), 2)

    masks = [2 ** (b + 1) for b in range(steps - 1)]
    peers = [
        (1 - odd) * flip(a) + odd * flip(b) for a, b in zip(masks, masks[::-1])
    ] + [flip(1)]
    feats = [lax.rem(mf + k, n_feat) for k in range(1, n_feat)]

    def rows_of(f):
        return pl.ds(pl.multiple_of(f * part, part), part)

    def cols_of(f):
        return pl.ds(pl.multiple_of(f * cols, cols), cols)

    def tile_at(t):
        return pl.ds(pl.multiple_of(t * TILE, TILE), TILE)

    def slots(a, b):
        return pl.ds(a * shard, (b - a) * shard)

    started = []

    def send(src, dst, s, r, dp, feat):
        copy = pltpu.make_async_remote_copy(
            src_ref=src, dst_ref=dst, send_sem=s, recv_sem=r,
            device_id=(dp, feat), device_id_type=MESH,
        )
        copy.start()
        started.append(copy)
        return copy

    def move(src, dst, s):
        copy = pltpu.make_async_copy(src, dst, s)
        copy.start()
        return copy

    def cot_copy(t, k, f):
        there = pl.ds(pl.multiple_of(f * cols + t * TILE, TILE), TILE)
        return pltpu.make_async_remote_copy(
            src_ref=cot_own.at[:, there], dst_ref=cot_v.at[rows_of(mf), tile_at(t)],
            send_sem=cot_s.at[t, k], recv_sem=cot_r.at[t, k],
            device_id=(me, f), device_id_type=MESH,
        )

    def cross_copy(t, k, f):
        there = pl.ds(pl.multiple_of(mf * cols + t * TILE, TILE), TILE)
        return pltpu.make_async_remote_copy(
            src_ref=cross.at[rows_of(f), tile_at(t)], dst_ref=cross_out.at[:, there],
            send_sem=cross_s.at[t, k], recv_sem=cross_r.at[t, k],
            device_id=(me, f), device_id_type=MESH,
        )

    def start_chunks(copy_of, lo, hi):
        @pl.loop(lo, hi)
        def _(t):
            for k, f in enumerate(feats):
                copy_of(t, k, f).start()

    barrier = pltpu.get_barrier_semaphore()
    for p in peers:
        pl.semaphore_signal(barrier, inc=1, device_id=(p, mf), device_id_type=MESH)
    for f in feats:
        pl.semaphore_signal(barrier, inc=1, device_id=(me, f), device_id_type=MESH)
    own = [
        move(down, d_full.at[slots(0, 1), :], local.at[0]),
        move(up, u_full.at[slots(0, 1), :], local.at[1]),
        move(cot, cot_own, local.at[2]),
    ]
    gate_v[...] = jnp.broadcast_to(gate[...], (128, rows)).T
    pl.semaphore_wait(barrier, steps + n_feat - 1)

    mid = 2 ** (steps - 1)
    half = mid // 2

    def swap(w, full, s, lo, hi, to, sem):
        return send(
            full.at[slots(lo, hi), :], full.at[slots(to, to + hi - lo), :],
            ag_s.at[w, sem], ag_r.at[w, sem], peers[s], mf)

    early = [None, None]

    def first_hop(w, full):
        return swap(w, full, 0, 0, 1, 1, 0)

    def middle_hops(w, full, hop):
        for s in range(1, steps - 1):
            hop.wait_recv()
            hop = swap(w, full, s, 0, 2 ** s, 2 ** s, s)
            if s == steps - 2:
                early[w] = swap(w, full, steps - 1, 0, half, mid, steps - 1)
        return hop

    def last_hop(w, full, hop):
        hop.wait_recv()
        return swap(w, full, steps - 1, half, mid, mid + half, steps)

    def spread_parts(which, total, outgoing, incoming):
        copies = []
        for k, f in enumerate(feats):
            outgoing[rows_of(f), :] = total[rows_of(f), :].astype(BF16)
            copies.append(send(
                outgoing.at[rows_of(f), :], incoming.at[k],
                sum_s.at[which, k], sum_r.at[which, k], me, f))
        return copies

    def share_sum(which, total, incoming, copies, result):
        value = total[rows_of(mf), :]
        for k, copy in enumerate(copies):
            copy.wait_recv()
            value = value + incoming[k].astype(F32)
        result[rows_of(mf), :] = value.astype(BF16)
        return [
            send(result.at[rows_of(mf), :], result.at[rows_of(mf), :],
                 all_s.at[which, k], all_r.at[which, k], me, f)
            for k, f in enumerate(feats)
        ]

    def wait_all(copies):
        for copy in copies:
            copy.wait_recv()

    def bias_send(s):
        return send(b_part, b_in.at[s], bias_s.at[s], bias_r.at[s], peers[s], mf)

    def bias_fold(s, copy):
        copy.wait()
        started[:] = [other for other in started if other is not copy]
        b_part[...] += b_in[s]

    own[0].wait()
    hop = first_hop(0, d_full)
    own[2].wait()
    start_chunks(cot_copy, 0, tiles // 2)
    hop = middle_hops(0, d_full, hop)
    late = last_hop(0, d_full, hop)
    own[1].wait()
    hop = first_hop(1, u_full)
    cot_v[rows_of(mf), :] = cot_own[:, cols_of(mf)]
    near, far = slots(0, mid), slots(mid, 2 * mid)
    h_part[:, near] = lax.dot_general(x[...], d_full[near, :], NT, preferred_element_type=F32)
    early[0].wait_recv()
    late.wait_recv()
    h_part[:, far] = lax.dot_general(x[...], d_full[far, :], NT, preferred_element_type=F32)
    parts = spread_parts(0, h_part, h_send, h_in)
    start_chunks(cot_copy, tiles // 2, tiles * 5 // 8)
    hop = middle_hops(1, u_full, hop)
    shares = share_sum(0, h_part, h_in, parts, low)
    start_chunks(cot_copy, tiles * 5 // 8, tiles)
    late = last_hop(1, u_full, hop)
    wait_all(shares)
    early[1].wait_recv()
    late.wait_recv()

    @pl.loop(0, tiles)
    def _(t):
        c = tile_at(t)
        proj = jnp.dot(low[...], u_full[:, c], preferred_element_type=F32)
        plus = 1.0 + (gate_v[:, :1] * proj + bias[:, c])
        one_scale[:, c] = plus
        cross[:, c] = (x[:, c].astype(F32) * plus).astype(BF16)

    start_chunks(cross_copy, 0, tiles // 4)
    cross_out[:, cols_of(mf)] = cross[rows_of(mf), :]

    g_part[...] = jnp.zeros_like(g_part)
    low_t[...] = low[...].astype(F32).T.astype(BF16)

    @pl.loop(0, tiles)
    def _(t):
        c = tile_at(t)
        for k, f in enumerate(feats):
            cot_copy(t, k, f).wait_recv()
        pre = cot_v[:, c].astype(F32) * x[:, c].astype(F32)
        b_part[:, c] = jnp.sum(pre.reshape(rows // 8, 8, TILE), axis=0)
        scaled = (gate_v[:, :1] * pre).astype(BF16)
        g_part[...] += lax.dot_general(scaled, u_full[:, c], NT, preferred_element_type=F32)
        terms = jnp.dot(low_t[...], scaled, preferred_element_type=F32)
        acc_up[:, c] = terms[: mid * shard]
        out_up[far, c] = terms[mid * shard :].astype(BF16)

    parts = spread_parts(1, g_part, g_send, g_in)
    start_chunks(cross_copy, tiles // 4, tiles // 2)

    def scatter(w, s, out, arriving):
        return send(
            out.at[slots(2 ** s, 2 ** (s + 1)), :], arriving.at[slots(2 ** s, 2 ** (s + 1)), :],
            rs_s.at[w, s], rs_r.at[w, s], peers[s], mf)

    def fold(s, copy, acc, out, arriving, result):
        copy.wait_recv()
        n = 2 ** s

        @pl.loop(0, tiles)
        def _(t):
            c = tile_at(t)
            total = acc[slots(0, n), c] + arriving[slots(n, 2 * n), c].astype(F32)
            if s == 0:
                result[:, c] = total
            else:
                acc[slots(0, n // 2), c] = total[: n // 2 * shard]
                out[slots(n // 2, n), c] = total[n // 2 * shard :].astype(BF16)

    ups = (acc_up, out_up, in_up, grad_up)
    downs = (acc_down, out_down, in_down, grad_down)
    bias_hop = bias_send(steps - 1)
    up_hop = scatter(0, steps - 1, out_up, in_up)

    shares = share_sum(1, g_part, g_in, parts, low_grad)
    start_chunks(cross_copy, tiles // 2, tiles)
    fold(steps - 1, up_hop, *ups)
    up_hop = scatter(0, steps - 2, out_up, in_up)
    wait_all(shares)
    low_t[...] = low_grad[...].astype(F32).T.astype(BF16)

    @pl.loop(0, tiles)
    def _(t):
        c = tile_at(t)
        terms = jnp.dot(low_t[...], x[:, c], preferred_element_type=F32)
        acc_down[:, c] = terms[: mid * shard]
        out_down[far, c] = terms[mid * shard :].astype(BF16)

    down_hop = scatter(1, steps - 1, out_down, in_down)
    bias_fold(steps - 1, bias_hop)
    bias_hop = bias_send(steps - 2)
    fold(steps - 1, down_hop, *downs)
    down_hop = scatter(1, steps - 2, out_down, in_down)

    @pl.loop(0, tiles)
    def _(t):
        c = tile_at(t)
        back = jnp.dot(low_grad[...], d_full[:, c], preferred_element_type=F32)
        grad_in[:, c] = (cot_v[:, c].astype(F32) * one_scale[:, c] + back).astype(BF16)

    for s in range(steps - 2, -1, -1):
        fold(s, up_hop, *ups)
        if s:
            up_hop = scatter(0, s - 1, out_up, in_up)
        fold(s, down_hop, *downs)
        if s:
            down_hop = scatter(1, s - 1, out_down, in_down)
        bias_fold(s, bias_hop)
        if s:
            bias_hop = bias_send(s - 1)
    grad_bias[...] = jnp.sum(b_part[...], axis=0, keepdims=True)

    @pl.loop(0, tiles)
    def _(t):
        for k, f in enumerate(feats):
            cross_copy(t, k, f).wait_recv()
            cross_copy(t, k, f).wait_send()
            cot_copy(t, k, f).wait_send()

    for copy in started:
        copy.wait_send()


def hand_over(*refs):
    count = (len(refs) - 2) // 3
    arrive, leave = refs[-2:]
    inward, outward = [], []
    for src, dst, held in zip(refs[:count], refs[count : 2 * count], refs[2 * count : -2]):
        rows = src.shape[0]
        pieces = 4 if rows % 64 == 0 else 1
        for n in range(pieces):
            at = pl.ds(n * (rows // pieces), rows // pieces)
            k = len(inward)
            inward.append(pltpu.make_async_copy(src.at[at, :], held.at[at, :], arrive.at[k]))
            outward.append(pltpu.make_async_copy(held.at[at, :], dst.at[at, :], leave.at[k]))
    for copy in inward:
        copy.start()
    for first, second in zip(inward, outward):
        first.wait()
        second.start()
    for copy in outward:
        copy.wait()


def placed(*values):
    anywhere = [pl.BlockSpec(memory_space=pl.ANY)] * len(values)
    return pl.pallas_call(
        hand_over,
        out_shape=tuple(jax.ShapeDtypeStruct(v.shape, v.dtype) for v in values),
        in_specs=anywhere,
        out_specs=tuple(anywhere),
        scratch_shapes=[pltpu.VMEM(v.shape, v.dtype) for v in values]
        + [pltpu.SemaphoreType.DMA((4 * len(values),))] * 2,
        compiler_params=pltpu.CompilerParams(vmem_limit_bytes=62 * 2 ** 20),
    )(*values)


def kernel_form(n_dp, n_feat, features, gate, bias, down_weight, up_weight, cotangent):
    rows, cols = features.shape
    shard = up_weight.shape[0]
    rank = shard * n_dp
    part = rows // n_feat
    steps = n_dp.bit_length() - 1
    vmem = pl.BlockSpec(memory_space=pltpu.VMEM)
    hbm = pl.BlockSpec(memory_space=pl.ANY)
    dma = pltpu.SemaphoreType.DMA
    others = n_feat - 1
    tiles = cols // TILE
    results = pl.pallas_call(
        functools.partial(kernel, n_dp, n_feat, steps),
        out_shape=(
            jax.ShapeDtypeStruct((part, cols * n_feat), BF16),
            jax.ShapeDtypeStruct((shard, cols), F32),
            jax.ShapeDtypeStruct((shard, cols), F32),
            jax.ShapeDtypeStruct((1, cols), F32),
            jax.ShapeDtypeStruct((rows, cols), BF16),
        ),
        in_specs=[vmem, hbm, hbm, hbm, vmem, vmem],
        out_specs=(vmem, vmem, vmem, vmem, vmem),
        scratch_shapes=[
            pltpu.VMEM((part, cols * n_feat), BF16),
            pltpu.VMEM((rows, cols), BF16),
            pltpu.VMEM((rank, cols), BF16),
            pltpu.VMEM((rank, cols), BF16),
            pltpu.VMEM((rows, cols), F32),
            pltpu.VMEM((rows, cols), BF16),
            pltpu.VMEM((rank, rows), BF16),
            pltpu.VMEM((rank // 2, cols), F32),
            pltpu.VMEM((rank // 2, cols), F32),
            pltpu.VMEM((rank, cols), BF16),
            pltpu.VMEM((rank, cols), BF16),
            pltpu.VMEM((rank, cols), BF16),
            pltpu.VMEM((rank, cols), BF16),
            pltpu.VMEM((rows, 128), F32),
            pltpu.VMEM((rows, rank), F32),
            pltpu.VMEM((rows, rank), BF16),
            pltpu.VMEM((others, part, rank), BF16),
            pltpu.VMEM((rows, rank), BF16),
            pltpu.VMEM((rows, rank), F32),
            pltpu.VMEM((rows, rank), BF16),
            pltpu.VMEM((others, part, rank), BF16),
            pltpu.VMEM((rows, rank), BF16),
            pltpu.VMEM((8, cols), F32),
            pltpu.VMEM((steps, 8, cols), F32),
            dma((tiles, others)), dma((tiles, others)),
            dma((2, steps + 1)), dma((2, steps + 1)),
            dma((2, others)), dma((2, others)),
            dma((2, others)), dma((2, others)),
            dma((tiles, others)), dma((tiles, others)),
            dma((2, steps)), dma((2, steps)),
            dma((steps,)), dma((steps,)),
            dma((3,)),
        ],
        compiler_params=pltpu.CompilerParams(
            collective_id=0, has_side_effects=True, vmem_limit_bytes=62 * 2 ** 20
        ),
        cost_estimate=pl.CostEstimate(
            flops=12 * rows * rank * cols, bytes_accessed=16 * rows * cols, transcendentals=0
        ),
    )(features, cotangent, down_weight.T, up_weight, gate[None, :], bias[None, :])
    cross_out, grad_up, grad_down, grad_bias, grad_in = placed(*results)
    return cross_out, grad_up, grad_down.T, grad_bias[0], grad_in


def solution(mesh):
    n_dp, n_feat = mesh.shape["dp"], mesh.shape["feat"]

    def on_device(features, gate, bias, down_weight, up_weight, cotangent):
        rows, cols = features.shape
        fits = (
            n_dp >= 4
            and n_dp & (n_dp - 1) == 0
            and n_feat > 1
            and up_weight.shape[0] % 16 == 0
            and rows % (16 * n_feat) == 0
            and cols % TILE == 0 and cols // TILE >= 8
        )
        args = (features, gate, bias, down_weight, up_weight, cotangent)
        return kernel_form(n_dp, n_feat, *args) if fits else plain_form(*args)

    in_specs = (
        P("dp", "feat"),
        P("dp"),
        P("feat"),
        P("feat", "dp"),
        P("dp", "feat"),
        P(("dp", "feat"), None),
    )
    out_specs = (
        P(("dp", "feat"), None),
        P("dp", "feat"),
        P("feat", "dp"),
        P("feat"),
        P("dp", "feat"),
    )
    return jax.shard_map(
        on_device, mesh=mesh, in_specs=in_specs, out_specs=out_specs, check_vma=False
    )
```

```python
import functools

import jax
import jax.numpy as jnp
from jax import lax
from jax.experimental import pallas as pl
from jax.experimental.pallas import tpu as pltpu
from jax.sharding import PartitionSpec as P

MESH = pl.DeviceIdType.MESH
F32 = jnp.float32
BF16 = jnp.bfloat16
NT = (((1,), (1,)), ((), ()))
TILE = 512


def rank_total(partial_value):
    return lax.psum(partial_value, "feat").astype(jnp.bfloat16)


def plain_form(features, gate, bias, down_weight, up_weight, cotangent):
    down_full, up_full = (
        lax.all_gather(down_weight, "dp", axis=1, tiled=True),
        lax.all_gather(up_weight, "dp", axis=0, tiled=True),
    )
    low = rank_total(jnp.dot(features, down_full, preferred_element_type=jnp.float32))
    proj = jnp.dot(low, up_full, preferred_element_type=jnp.float32)
    scale = gate[:, None] * proj + bias[None, :]
    xfloat = features.astype(jnp.float32)
    cross = (xfloat * (1.0 + scale)).astype(jnp.bfloat16)
    cross_out = lax.all_to_all(cross, "feat", split_axis=0, concat_axis=1, tiled=True)
    upstream = lax.all_to_all(cotangent, "feat", split_axis=1, concat_axis=0, tiled=True).astype(
        jnp.float32
    )
    pre_grad = upstream * xfloat
    bias_terms = jnp.sum(pre_grad, axis=0)
    gated_grad = (gate[:, None] * pre_grad).astype(jnp.bfloat16)
    contract_first = (((0,), (0,)), ((), ()))
    rank_grad = lax.dot_general(gated_grad, up_full, NT, preferred_element_type=jnp.float32)
    low_grad = rank_total(rank_grad)
    grad_up = lax.psum_scatter(
        lax.dot_general(low, gated_grad, contract_first, preferred_element_type=jnp.float32),
        "dp",
        scatter_dimension=0,
        tiled=True,
    )
    down_terms = lax.dot_general(
        features, low_grad, contract_first, preferred_element_type=jnp.float32
    )
    grad_down = lax.psum_scatter(down_terms, "dp", scatter_dimension=1, tiled=True)
    grad_bias = lax.psum(bias_terms, "dp")
    back = lax.dot_general(low_grad, down_full, NT, preferred_element_type=jnp.float32)
    grad_in = (upstream * (1.0 + scale) + back).astype(jnp.bfloat16)
    return (cross_out, grad_up, grad_down, grad_bias, grad_in)


def kernel(
    n_dp, n_feat, steps,
    x, cot, down, up, gate, bias,
    cross_out, grad_up, grad_down, grad_bias, grad_in,
    cot_own, cot_v, d_full, u_full, one_scale, cross,
    low_t, acc_up, acc_down, out_up, out_down, in_up, in_down,
    gate_v, h_part, h_send, h_in, low, g_part, g_send, g_in, low_grad,
    b_part, b_in,
    cot_s, cot_r, ag_s, ag_r, sum_s, sum_r, all_s, all_r,
    cross_s, cross_r, rs_s, rs_r, bias_s, bias_r, local,
):
    me = lax.axis_index("dp")
    mf = lax.axis_index("feat")
    rows, cols = x.shape
    part = rows // n_feat
    rank = u_full.shape[0]
    shard = rank // n_dp
    tiles = cols // TILE
    odd = lax.rem(me, 2)

    def flip(mask):
        return me + mask - 2 * mask * lax.rem(lax.div(me, mask), 2)

    masks = [2 ** (b + 1) for b in range(steps - 1)]
    peers = [
        (1 - odd) * flip(a) + odd * flip(b) for a, b in zip(masks, masks[::-1])
    ] + [flip(1)]
    feats = [lax.rem(mf + k, n_feat) for k in range(1, n_feat)]

    def rows_of(f):
        return pl.ds(pl.multiple_of(f * part, part), part)

    def cols_of(f):
        return pl.ds(pl.multiple_of(f * cols, cols), cols)

    def tile_at(t):
        return pl.ds(pl.multiple_of(t * TILE, TILE), TILE)

    def slots(a, b):
        return pl.ds(a * shard, (b - a) * shard)

    started = []

    def send(src, dst, s, r, dp, feat):
        copy = pltpu.make_async_remote_copy(
            src_ref=src, dst_ref=dst, send_sem=s, recv_sem=r,
            device_id=(dp, feat), device_id_type=MESH,
        )
        copy.start()
        started.append(copy)
        return copy

    def move(src, dst, s):
        copy = pltpu.make_async_copy(src, dst, s)
        copy.start()
        return copy

    def cot_copy(t, k, f):
        there = pl.ds(pl.multiple_of(f * cols + t * TILE, TILE), TILE)
        return pltpu.make_async_remote_copy(
            src_ref=cot_own.at[:, there], dst_ref=cot_v.at[rows_of(mf), tile_at(t)],
            send_sem=cot_s.at[t, k], recv_sem=cot_r.at[t, k],
            device_id=(me, f), device_id_type=MESH,
        )

    def cross_copy(t, k, f):
        there = pl.ds(pl.multiple_of(mf * cols + t * TILE, TILE), TILE)
        return pltpu.make_async_remote_copy(
            src_ref=cross.at[rows_of(f), tile_at(t)], dst_ref=cross_out.at[:, there],
            send_sem=cross_s.at[t, k], recv_sem=cross_r.at[t, k],
            device_id=(me, f), device_id_type=MESH,
        )

    def start_chunks(copy_of, lo, hi):
        @pl.loop(lo, hi)
        def _(t):
            for k, f in enumerate(feats):
                copy_of(t, k, f).start()

    barrier = pltpu.get_barrier_semaphore()
    for p in peers:
        pl.semaphore_signal(barrier, inc=1, device_id=(p, mf), device_id_type=MESH)
    for f in feats:
        pl.semaphore_signal(barrier, inc=1, device_id=(me, f), device_id_type=MESH)
    own = [
        move(down, d_full.at[slots(0, 1), :], local.at[0]),
        move(up, u_full.at[slots(0, 1), :], local.at[1]),
        move(cot, cot_own, local.at[2]),
    ]
    gate_v[...] = jnp.broadcast_to(gate[...], (128, rows)).T
    pl.semaphore_wait(barrier, steps + n_feat - 1)

    mid = 2 ** (steps - 1)
    half = mid // 2

    def swap(w, full, s, lo, hi, to, sem):
        return send(
            full.at[slots(lo, hi), :], full.at[slots(to, to + hi - lo), :],
            ag_s.at[w, sem], ag_r.at[w, sem], peers[s], mf)

    early = [None, None]

    def first_hop(w, full):
        return swap(w, full, 0, 0, 1, 1, 0)

    def middle_hops(w, full, hop):
        for s in range(1, steps - 1):
            hop.wait_recv()
            hop = swap(w, full, s, 0, 2 ** s, 2 ** s, s)
            if s == steps - 2:
                early[w] = swap(w, full, steps - 1, 0, half, mid, steps - 1)
        return hop

    def last_hop(w, full, hop):
        hop.wait_recv()
        return swap(w, full, steps - 1, half, mid, mid + half, steps)

    def spread_parts(which, total, outgoing, incoming):
        copies = []
        for k, f in enumerate(feats):
            outgoing[rows_of(f), :] = total[rows_of(f), :].astype(BF16)
            copies.append(send(
                outgoing.at[rows_of(f), :], incoming.at[k],
                sum_s.at[which, k], sum_r.at[which, k], me, f))
        return copies

    def share_sum(which, total, incoming, copies, result):
        value = total[rows_of(mf), :]
        for k, copy in enumerate(copies):
            copy.wait_recv()
            value = value + incoming[k].astype(F32)
        result[rows_of(mf), :] = value.astype(BF16)
        return [
            send(result.at[rows_of(mf), :], result.at[rows_of(mf), :],
                 all_s.at[which, k], all_r.at[which, k], me, f)
            for k, f in enumerate(feats)
        ]

    def wait_all(copies):
        for copy in copies:
            copy.wait_recv()

    def bias_send(s):
        return send(b_part, b_in.at[s], bias_s.at[s], bias_r.at[s], peers[s], mf)

    def bias_fold(s, copy):
        copy.wait()
        started[:] = [other for other in started if other is not copy]
        b_part[...] += b_in[s]

    own[0].wait()
    hop = first_hop(0, d_full)
    own[2].wait()
    start_chunks(cot_copy, 0, tiles // 2)
    hop = middle_hops(0, d_full, hop)
    late = last_hop(0, d_full, hop)
    own[1].wait()
    hop = first_hop(1, u_full)
    cot_v[rows_of(mf), :] = cot_own[:, cols_of(mf)]
    near, far = slots(0, mid), slots(mid, 2 * mid)
    h_part[:, near] = lax.dot_general(x[...], d_full[near, :], NT, preferred_element_type=F32)
    early[0].wait_recv()
    late.wait_recv()
    h_part[:, far] = lax.dot_general(x[...], d_full[far, :], NT, preferred_element_type=F32)
    parts = spread_parts(0, h_part, h_send, h_in)
    start_chunks(cot_copy, tiles // 2, tiles * 5 // 8)
    hop = middle_hops(1, u_full, hop)
    shares = share_sum(0, h_part, h_in, parts, low)
    start_chunks(cot_copy, tiles * 5 // 8, tiles)
    late = last_hop(1, u_full, hop)
    wait_all(shares)
    early[1].wait_recv()
    late.wait_recv()

    @pl.loop(0, tiles)
    def _(t):
        c = tile_at(t)
        proj = jnp.dot(low[...], u_full[:, c], preferred_element_type=F32)
        plus = 1.0 + (gate_v[:, :1] * proj + bias[:, c])
        one_scale[:, c] = plus
        cross[:, c] = (x[:, c].astype(F32) * plus).astype(BF16)

    start_chunks(cross_copy, 0, tiles // 4)
    cross_out[:, cols_of(mf)] = cross[rows_of(mf), :]

    g_part[...] = jnp.zeros_like(g_part)
    low_t[...] = low[...].astype(F32).T.astype(BF16)

    @pl.loop(0, tiles)
    def _(t):
        c = tile_at(t)
        for k, f in enumerate(feats):
            cot_copy(t, k, f).wait_recv()
        pre = cot_v[:, c].astype(F32) * x[:, c].astype(F32)
        b_part[:, c] = jnp.sum(pre.reshape(rows // 8, 8, TILE), axis=0)
        scaled = (gate_v[:, :1] * pre).astype(BF16)
        g_part[...] += lax.dot_general(scaled, u_full[:, c], NT, preferred_element_type=F32)
        terms = jnp.dot(low_t[...], scaled, preferred_element_type=F32)
        acc_up[:, c] = terms[: mid * shard]
        out_up[far, c] = terms[mid * shard :].astype(BF16)

    parts = spread_parts(1, g_part, g_send, g_in)
    start_chunks(cross_copy, tiles // 4, tiles // 2)

    def scatter(w, s, out, arriving, lo, hi):
        block = (slots(2 ** s, 2 ** (s + 1)), pl.ds(lo * TILE, (hi - lo) * TILE))
        return send(
            out.at[block], arriving.at[block], rs_s.at[w, s], rs_r.at[w, s], peers[s], mf)

    def fold(s, copy, lo, hi, acc, out, arriving, result):
        copy.wait_recv()
        n = 2 ** s

        @pl.loop(lo, hi)
        def _(t):
            c = tile_at(t)
            total = acc[slots(0, n), c] + arriving[slots(n, 2 * n), c].astype(F32)
            if s == 0:
                result[:, c] = total
            else:
                acc[slots(0, n // 2), c] = total[: n // 2 * shard]
                out[slots(n // 2, n), c] = total[n // 2 * shard :].astype(BF16)

    ups = (acc_up, out_up, in_up, grad_up)
    downs = (acc_down, out_down, in_down, grad_down)
    bias_hop = bias_send(steps - 1)
    up_hop = scatter(0, steps - 1, out_up, in_up, 0, tiles)

    shares = share_sum(1, g_part, g_in, parts, low_grad)
    start_chunks(cross_copy, tiles // 2, tiles)
    fold(steps - 1, up_hop, 0, tiles, *ups)
    up_hop = scatter(0, steps - 2, out_up, in_up, 0, tiles)
    wait_all(shares)
    low_t[...] = low_grad[...].astype(F32).T.astype(BF16)

    halves = ((1, 0, tiles // 2), (2, tiles // 2, tiles))
    down_hops = {}
    for w, lo, hi in halves:

        @pl.loop(lo, hi)
        def _(t):
            c = tile_at(t)
            terms = jnp.dot(low_t[...], x[:, c], preferred_element_type=F32)
            acc_down[:, c] = terms[: mid * shard]
            out_down[far, c] = terms[mid * shard :].astype(BF16)

        down_hops[w] = scatter(w, steps - 1, out_down, in_down, lo, hi)

    def down_step(s):
        for w, lo, hi in halves:
            fold(s, down_hops[w], lo, hi, *downs)
            if s:
                down_hops[w] = scatter(w, s - 1, out_down, in_down, lo, hi)

    down_step(steps - 1)
    bias_fold(steps - 1, bias_hop)
    bias_hop = bias_send(steps - 2)

    @pl.loop(0, tiles)
    def _(t):
        c = tile_at(t)
        back = jnp.dot(low_grad[...], d_full[:, c], preferred_element_type=F32)
        grad_in[:, c] = (cot_v[:, c].astype(F32) * one_scale[:, c] + back).astype(BF16)

    for s in range(steps - 2, -1, -1):
        fold(s, up_hop, 0, tiles, *ups)
        if s:
            up_hop = scatter(0, s - 1, out_up, in_up, 0, tiles)
        down_step(s)
        bias_fold(s, bias_hop)
        if s:
            bias_hop = bias_send(s - 1)
    grad_bias[...] = jnp.sum(b_part[...], axis=0, keepdims=True)

    @pl.loop(0, tiles)
    def _(t):
        for k, f in enumerate(feats):
            cross_copy(t, k, f).wait_recv()
            cross_copy(t, k, f).wait_send()
            cot_copy(t, k, f).wait_send()

    for copy in started:
        copy.wait_send()


def hand_over(*refs):
    count = (len(refs) - 2) // 3
    arrive, leave = refs[-2:]
    inward, outward = [], []
    for src, dst, held in zip(refs[:count], refs[count : 2 * count], refs[2 * count : -2]):
        rows = src.shape[0]
        pieces = 4 if rows % 64 == 0 else 1
        for n in range(pieces):
            at = pl.ds(n * (rows // pieces), rows // pieces)
            k = len(inward)
            inward.append(pltpu.make_async_copy(src.at[at, :], held.at[at, :], arrive.at[k]))
            outward.append(pltpu.make_async_copy(held.at[at, :], dst.at[at, :], leave.at[k]))
    for copy in inward:
        copy.start()
    for first, second in zip(inward, outward):
        first.wait()
        second.start()
    for copy in outward:
        copy.wait()


def placed(*values):
    anywhere = [pl.BlockSpec(memory_space=pl.ANY)] * len(values)
    return pl.pallas_call(
        hand_over,
        out_shape=tuple(jax.ShapeDtypeStruct(v.shape, v.dtype) for v in values),
        in_specs=anywhere,
        out_specs=tuple(anywhere),
        scratch_shapes=[pltpu.VMEM(v.shape, v.dtype) for v in values]
        + [pltpu.SemaphoreType.DMA((4 * len(values),))] * 2,
        compiler_params=pltpu.CompilerParams(vmem_limit_bytes=62 * 2 ** 20),
    )(*values)


def kernel_form(n_dp, n_feat, features, gate, bias, down_weight, up_weight, cotangent):
    rows, cols = features.shape
    shard = up_weight.shape[0]
    rank = shard * n_dp
    part = rows // n_feat
    steps = n_dp.bit_length() - 1
    vmem = pl.BlockSpec(memory_space=pltpu.VMEM)
    hbm = pl.BlockSpec(memory_space=pl.ANY)
    dma = pltpu.SemaphoreType.DMA
    others = n_feat - 1
    tiles = cols // TILE
    results = pl.pallas_call(
        functools.partial(kernel, n_dp, n_feat, steps),
        out_shape=(
            jax.ShapeDtypeStruct((part, cols * n_feat), BF16),
            jax.ShapeDtypeStruct((shard, cols), F32),
            jax.ShapeDtypeStruct((shard, cols), F32),
            jax.ShapeDtypeStruct((1, cols), F32),
            jax.ShapeDtypeStruct((rows, cols), BF16),
        ),
        in_specs=[vmem, hbm, hbm, hbm, vmem, vmem],
        out_specs=(vmem, vmem, vmem, vmem, vmem),
        scratch_shapes=[
            pltpu.VMEM((part, cols * n_feat), BF16),
            pltpu.VMEM((rows, cols), BF16),
            pltpu.VMEM((rank, cols), BF16),
            pltpu.VMEM((rank, cols), BF16),
            pltpu.VMEM((rows, cols), F32),
            pltpu.VMEM((rows, cols), BF16),
            pltpu.VMEM((rank, rows), BF16),
            pltpu.VMEM((rank // 2, cols), F32),
            pltpu.VMEM((rank // 2, cols), F32),
            pltpu.VMEM((rank, cols), BF16),
            pltpu.VMEM((rank, cols), BF16),
            pltpu.VMEM((rank, cols), BF16),
            pltpu.VMEM((rank, cols), BF16),
            pltpu.VMEM((rows, 128), F32),
            pltpu.VMEM((rows, rank), F32),
            pltpu.VMEM((rows, rank), BF16),
            pltpu.VMEM((others, part, rank), BF16),
            pltpu.VMEM((rows, rank), BF16),
            pltpu.VMEM((rows, rank), F32),
            pltpu.VMEM((rows, rank), BF16),
            pltpu.VMEM((others, part, rank), BF16),
            pltpu.VMEM((rows, rank), BF16),
            pltpu.VMEM((8, cols), F32),
            pltpu.VMEM((steps, 8, cols), F32),
            dma((tiles, others)), dma((tiles, others)),
            dma((2, steps + 1)), dma((2, steps + 1)),
            dma((2, others)), dma((2, others)),
            dma((2, others)), dma((2, others)),
            dma((tiles, others)), dma((tiles, others)),
            dma((3, steps)), dma((3, steps)),
            dma((steps,)), dma((steps,)),
            dma((3,)),
        ],
        compiler_params=pltpu.CompilerParams(
            collective_id=0, has_side_effects=True, vmem_limit_bytes=62 * 2 ** 20
        ),
        cost_estimate=pl.CostEstimate(
            flops=12 * rows * rank * cols, bytes_accessed=16 * rows * cols, transcendentals=0
        ),
    )(features, cotangent, down_weight.T, up_weight, gate[None, :], bias[None, :])
    cross_out, grad_up, grad_down, grad_bias, grad_in = placed(*results)
    return cross_out, grad_up, grad_down.T, grad_bias[0], grad_in


def solution(mesh):
    n_dp, n_feat = mesh.shape["dp"], mesh.shape["feat"]

    def on_device(features, gate, bias, down_weight, up_weight, cotangent):
        rows, cols = features.shape
        fits = (
            n_dp >= 4
            and n_dp & (n_dp - 1) == 0
            and n_feat > 1
            and up_weight.shape[0] % 16 == 0
            and rows % (16 * n_feat) == 0
            and cols % TILE == 0 and cols // TILE >= 8
        )
        args = (features, gate, bias, down_weight, up_weight, cotangent)
        return kernel_form(n_dp, n_feat, *args) if fits else plain_form(*args)

    in_specs = (
        P("dp", "feat"),
        P("dp"),
        P("feat"),
        P("feat", "dp"),
        P("dp", "feat"),
        P(("dp", "feat"), None),
    )
    out_specs = (
        P(("dp", "feat"), None),
        P("dp", "feat"),
        P("feat", "dp"),
        P("feat"),
        P("dp", "feat"),
    )
    return jax.shard_map(
        on_device, mesh=mesh, in_specs=in_specs, out_specs=out_specs, check_vma=False
    )
```
